32 devices in a mesh: farm: 2 (over x), body: 16 (over z, y, core).
Axes of the slice: x: 2, y: 2, z: 4, core: 2. Of those that a mesh axis runs over, the one named last changes fastest.
Arguments:
- incident: float32 [32, 2, 16, 768], P(('farm', 'body')), parts along dimension 0, may hold values from -6 to 6
- self_inverse: float32 [32, 2, 768, 768], P(('farm', 'body')), parts along dimension 0
- cross_blocks: float32 [32, 4, 2, 768, 768], P(('farm', 'body')), parts along dimension 0, may hold values from -0.046875 to 0.046875
- neighbours: int32 [32, 4], P(('farm', 'body')), parts along dimension 0, may hold values from -1 to 15, as said below
- panel_weight: float32 [32, 768], P(('farm', 'body')), parts along dimension 0, may hold values from -0.0546875 to 0.0546875
Outputs:
- sources: float32 [32, 2, 16, 768], P(('farm', 'body')), parts along dimension 0
- farm_force: float32 [2, 2, 16], P('farm'), parts along dimension 0
The draws below stay inside these ranges and needn't reach their ends.
There are 2 independent parts, one for each index of `farm`. The reference program is written for one: setup_inputs(seed, part) draws one part's arguments, and reference() takes and returns one part's arrays. A program takes and returns all parts, laid end to end along the dimension named above; each array names one. Nothing has to cross between parts.
Inputs may be any that keep to these rules, and one draw needn't show every extreme that they name: `neighbours`: each row names distinct bodies other than its own, each within 8 positions of it around the closed loop of 16 bodies; some body names the body exactly 8 positions away.
All inputs are finite; a program needn't handle non-finite values.
Results may differ from the reference program's by a relative error of at most 0.0003.
Values sent between devices are 32-bit elements; how exact they have to be, the bound alone decides.
A program may use at most 128 MiB of HBM per device.

```python
import math
import jax
import jax.numpy as jnp
from jax import lax

PANELS = 768
HEADINGS = 16
SLOTS = 4
ITERS = 6
BODIES = 16
REACH = 8


def draw_self_inverse(key, part):
    key_off, key_diag = jax.random.split(jax.random.fold_in(key, 11))
    shape = (BODIES, 2, PANELS, PANELS)
    off = jax.random.normal(key_off, shape, jnp.float32) * (0.3 / math.sqrt(PANELS))
    diag = jax.random.uniform(key_diag, (BODIES, PANELS), jnp.float32, 0.5, 1.5)
    eye = jnp.arange(PANELS)[:, None] == jnp.arange(PANELS)[None, :]
    real_part = off[:, 0] + jnp.where(eye[None], diag[:, :, None], 0.0)
    return jnp.stack([real_part, off[:, 1]], axis=1).astype(jnp.float32)


def draw_neighbours(key, part):
    key_score, key_row, key_keep = jax.random.split(jax.random.fold_in(key, 23), 3)
    steps_up = jnp.arange(1, REACH + 1, dtype=jnp.int32)
    steps_down = -jnp.arange(1, REACH, dtype=jnp.int32)
    candidates = jnp.concatenate([steps_up, steps_down])
    width = 2 * REACH - 1
    scores = jax.random.randint(key_score, (BODIES, width), 0, 1 << 20) * width + jnp.arange(width, dtype=jnp.int32)[None]
    order = jnp.argsort(scores, axis=1, stable=True)[:, :SLOTS]
    offsets = candidates[order]
    special = jnp.array([REACH, 1, -1, 2], dtype=jnp.int32)[:SLOTS]
    chosen = jax.random.randint(key_row, (), 0, BODIES)
    is_chosen = (jnp.arange(BODIES) == chosen)[:, None]
    offsets = jnp.where(is_chosen, special[None], offsets)
    keep = (jax.random.randint(key_keep, (BODIES, SLOTS), 0, 4) > 0) | is_chosen
    source_index = (jnp.arange(BODIES, dtype=jnp.int32)[:, None] + offsets) % BODIES
    return jnp.where(keep, source_index, -1).astype(jnp.int32)


def block_levels(own_key, shape, shards, low, high):
    loudness = 1.0
    for axis_at, parts in shards:
        steps = jax.random.uniform(jax.random.fold_in(jax.random.fold_in(own_key, 6), axis_at), (parts,), jnp.float32, low / len(shards), high / len(shards))
        loudness = loudness * jnp.repeat(jnp.exp(steps), shape[axis_at] // parts).reshape((-1,) + (1,) * (len(shape) - 1 - axis_at))
    return loudness


def centred(rng, shape, deviation, bound, cuts=(), held_as=jnp.bfloat16):
    level = block_levels(rng, shape, cuts, -0.22, 0.18) if cuts else 1.0
    values = jax.random.normal(rng, shape, jnp.float32) * deviation * level
    return jnp.minimum(jnp.maximum(values, -bound), bound).astype(held_as)


def setup_inputs(seed: int = 0, part: int = 0) -> dict:
    keys = jax.random.split(jax.random.key(seed), 6)
    own_keys = jax.random.split(jax.random.fold_in(keys[5], part), 6)
    incident = centred(own_keys[0], (BODIES, 2, HEADINGS, PANELS), 1.0, 6.0, ((0, 16),), jnp.float32)
    self_inverse = draw_self_inverse(jax.random.fold_in(jax.random.fold_in(keys[5], part), 71), part)
    cross_blocks = centred(own_keys[2], (BODIES, SLOTS, 2, PANELS, PANELS), (25 * PANELS) ** -0.5, 0.046875, ((0, 16),), jnp.float32)
    neighbours = draw_neighbours(jax.random.fold_in(jax.random.fold_in(keys[5], part), 71), part)
    panel_weight = centred(own_keys[4], (BODIES, PANELS), (BODIES * PANELS) ** -0.5, 0.0546875, ((0, 16),), jnp.float32)
    return dict(incident=incident, self_inverse=self_inverse, cross_blocks=cross_blocks, neighbours=neighbours, panel_weight=panel_weight)


def complex_apply(matrix, field):
    heads = field.shape[1]
    stacked = field.reshape(2 * heads, field.shape[2])
    dims = (((1,), (1,)), ((), ()))
    real_part = lax.dot_general(stacked, matrix[0], dims, precision=lax.Precision.HIGHEST)
    imag_part = lax.dot_general(stacked, matrix[1], dims, precision=lax.Precision.HIGHEST)
    return jnp.stack([real_part[:heads] - imag_part[heads:], real_part[heads:] + imag_part[:heads]])


def reference(incident, self_inverse, cross_blocks, neighbours, panel_weight):
    live = neighbours >= 0
    safe = jnp.where(live, neighbours, 0).astype(jnp.int32)
    sources = lax.map(lambda pair: complex_apply(pair[0], pair[1]), (self_inverse, incident))
    for sweep in range(ITERS):
        previous = sources

        def update(items):
            inverse_one, blocks, field, index_row, flag_row = items
            total = field
            for slot in range(SLOTS):
                other = lax.dynamic_index_in_dim(previous, index_row[slot], 0, keepdims=False)
                total = total - jnp.where(flag_row[slot], complex_apply(blocks[slot], other), 0.0)
            return complex_apply(inverse_one, total)

        sources = lax.map(update, (self_inverse, cross_blocks, incident, safe, live))
    force = jnp.einsum("bp,bchp->ch", panel_weight, sources, precision=lax.Precision.HIGHEST)
    return sources, force[None]
```

```python
import functools

import jax
import jax.numpy as jnp
from jax import lax
from jax.experimental import pallas as pl
from jax.experimental.pallas import tpu as pltpu
from jax.sharding import PartitionSpec as P

ITERS = 6
F32 = jnp.float32
BF16 = jnp.bfloat16


def flip(index, bits):
    bit = 1
    while bit <= bits:
        if bits & bit:
            index = index + bit - 2 * bit * ((index // bit) % 2)
        bit *= 2
    return index


def halves(value):
    high = value.astype(BF16)
    return high, (value - high.astype(F32)).astype(BF16)


def dot_t(left, right):
    return lax.dot_general(left, right, (((1,), (1,)), ((), ())), preferred_element_type=F32)


def put_field(lhs, column, value, heads):
    rows, panels = value.shape
    high, low = halves(value)
    high_t = jnp.concatenate([-high[heads:], high[:heads]], axis=0)
    low_t = jnp.concatenate([-low[heads:], low[:heads]], axis=0)
    lhs[0:rows, column : column + panels] = high
    lhs[rows : 2 * rows, column : column + panels] = low
    lhs[0:rows, column + panels : column + 2 * panels] = high_t
    lhs[rows : 2 * rows, column + panels : column + 2 * panels] = low_t


def multiply(lhs, depth, high, low, out, rows):
    panels = out.shape[1]
    tile = 256
    for start in range(0, panels, tile):
        both = dot_t(lhs[:, 0:depth], high[start : start + tile, :])
        small = dot_t(lhs[0:rows, 0:depth], low[start : start + tile, :])
        out[:, start : start + tile] = both[:rows] + both[rows:] + small


def kernel(
    bodies, slots, heads, panels,
    neighbours, incident, inverse, blocks, weight,
    out, force,
    stage, inv_high, inv_low, cross_high, cross_low, even, odd, lhs, product, shares,
    load_sem, send_sem, recv_sem, share_send, share_recv,
):
    rows = 2 * heads
    me = lax.axis_index("body")
    depth_z = bodies // 4
    gathered = (even, odd)

    def load(index):
        source = inverse.at[0, index] if index < 2 else blocks.at[0, (index - 2) // 2, (index - 2) % 2]
        return pltpu.make_async_copy(source, stage.at[index], load_sem.at[index])

    for index in range(2 + 2 * slots):
        load(index).start()

    barrier = pltpu.get_barrier_semaphore()
    for bits in range(1, bodies):
        pl.semaphore_signal(barrier, inc=1, device_id={"body": flip(me, bits)})

    def split(index, high, low, column):
        load(index).wait()

        @pl.loop(0, panels // 64)
        def _(step):
            at = pl.ds(pl.multiple_of(step * 64, 64), 64)
            upper, lower = halves(stage[index, at, :])
            high[at, column : column + panels] = upper
            low[at, column : column + panels] = lower

    def send(parity, bits, target, index):
        slot = flip(me, bits)
        return pltpu.make_async_remote_copy(
            src_ref=gathered[parity].at[slot],
            dst_ref=gathered[parity].at[slot],
            send_sem=send_sem.at[index],
            recv_sem=recv_sem.at[parity, slot],
            device_id={"body": flip(me, target)},
        )

    own = [(0, 2), (0, 1)] + [(0, 4 * d) for d in range(1, depth_z)]
    relay = [(2, [1])]
    for d in range(1, depth_z):
        relay.append((4 * d, [2, 1]))
        relay.append((4 * d + 2, [1]))
    every = own + [(slot, target) for slot, targets in relay for target in targets]

    def start_own(parity):
        for index, (slot, target) in enumerate(own):
            send(parity, slot, target, index).start()

    def wait_in(parity, bits):
        slot = flip(me, bits)
        pltpu.make_async_remote_copy(
            src_ref=gathered[parity].at[slot],
            dst_ref=gathered[parity].at[slot],
            send_sem=send_sem.at[0],
            recv_sem=recv_sem.at[parity, slot],
            device_id={"body": flip(me, 1)},
        ).wait_recv()

    def finish_gather(parity):
        index = len(own)
        for slot, targets in relay:
            wait_in(parity, slot)
            for target in targets:
                send(parity, slot, target, index).start()
                index += 1
        for d in range(depth_z):
            wait_in(parity, 4 * d + 1)
            wait_in(parity, 4 * d + 3)

    def wait_sends(parity):
        for index, (slot, target) in enumerate(every):
            send(parity, slot, target, index).wait_send()

    field = incident[0].reshape(rows, panels)
    for part in range(2):
        split(part, inv_high, inv_low, part * panels)
    put_field(lhs, 0, field, heads)
    multiply(lhs, 2 * panels, inv_high, inv_low, product, rows)
    even[me] = product[...]
    pl.semaphore_wait(barrier, bodies - 1)
    start_own(0)
    for part in range(2 * slots):
        split(2 + part, cross_high, cross_low, part * panels)

    def sweep(parity):
        finish_gather(parity)
        for slot in range(slots):
            name = neighbours[0, slot]
            value = gathered[parity][jnp.maximum(name, 0)]
            put_field(lhs, 2 * slot * panels, jnp.where(name >= 0, value, 0.0), heads)
        multiply(lhs, 2 * slots * panels, cross_high, cross_low, product, rows)
        put_field(lhs, 0, incident[0].reshape(rows, panels) - product[...], heads)
        multiply(lhs, 2 * panels, inv_high, inv_low, product, rows)
        wait_sends(parity)

    @pl.loop(0, ITERS // 2)
    def _(pair):
        sweep(0)
        odd[me] = product[...]
        start_own(1)
        sweep(1)

        @pl.when(pair < ITERS // 2 - 1)
        def _():
            even[me] = product[...]
            start_own(0)

    final = product[...]
    out[0] = final.reshape(2, heads, panels)
    scale = jnp.broadcast_to(weight[...], (8, panels))
    sums = [
        lax.dot_general(
            scale, final[c * heads : (c + 1) * heads], (((1,), (1,)), ((), ())),
            precision=lax.Precision.HIGHEST, preferred_element_type=F32,
        )
        for c in range(2)
    ]
    row = lax.broadcasted_iota(jnp.int32, (8, heads), 0)
    shares[me] = jnp.zeros((8, 128), F32)
    shares[me, :, 0:heads] = jnp.where(row == 0, sums[0], sums[1])

    def share(bits):
        return pltpu.make_async_remote_copy(
            src_ref=shares.at[me],
            dst_ref=shares.at[me],
            send_sem=share_send.at[bits],
            recv_sem=share_recv.at[bits],
            device_id={"body": flip(me, bits)},
        )

    def share_in(bits):
        slot = flip(me, bits)
        return pltpu.make_async_remote_copy(
            src_ref=shares.at[slot],
            dst_ref=shares.at[slot],
            send_sem=share_send.at[bits],
            recv_sem=share_recv.at[bits],
            device_id={"body": slot},
        )

    for bits in range(1, bodies):
        share(bits).start()
    for bits in range(1, bodies):
        share_in(bits).wait_recv()
    total = shares[0]
    for other in range(1, bodies):
        total = total + shares[other]
    force[0] = total[0:2, 0:heads]
    for bits in range(1, bodies):
        share(bits).wait_send()


def solution(mesh):
    bodies = mesh.shape["body"]

    def step(incident, self_inverse, cross_blocks, neighbours, panel_weight):
        heads, panels = incident.shape[2:]
        slots = neighbours.shape[1]
        rows = 2 * heads
        vmem = pl.BlockSpec(memory_space=pltpu.VMEM)
        anywhere = pl.BlockSpec(memory_space=pl.ANY)
        copies = 2 * bodies
        return pl.pallas_call(
            functools.partial(kernel, bodies, slots, heads, panels),
            out_shape=(
                jax.ShapeDtypeStruct(incident.shape, F32),
                jax.ShapeDtypeStruct((1, 2, heads), F32),
            ),
            in_specs=[pl.BlockSpec(memory_space=pltpu.SMEM), vmem, anywhere, anywhere, vmem],
            out_specs=(vmem, vmem),
            scratch_shapes=[
                pltpu.VMEM((2 + 2 * slots, panels, panels), F32),
                pltpu.VMEM((panels, 2 * panels), BF16),
                pltpu.VMEM((panels, 2 * panels), BF16),
                pltpu.VMEM((panels, 2 * slots * panels), BF16),
                pltpu.VMEM((panels, 2 * slots * panels), BF16),
                pltpu.VMEM((bodies, rows, panels), F32),
                pltpu.VMEM((bodies, rows, panels), F32),
                pltpu.VMEM((2 * rows, 2 * slots * panels), BF16),
                pltpu.VMEM((rows, panels), F32),
                pltpu.VMEM((bodies, 8, 128), F32),
                pltpu.SemaphoreType.DMA((2 + 2 * slots,)),
                pltpu.SemaphoreType.DMA((copies,)),
                pltpu.SemaphoreType.DMA((2, bodies)),
                pltpu.SemaphoreType.DMA((bodies,)),
                pltpu.SemaphoreType.DMA((bodies,)),
            ],
            compiler_params=pltpu.CompilerParams(
                collective_id=0, has_side_effects=True, vmem_limit_bytes=60 * 1024 * 1024
            ),
        )(neighbours, incident, self_inverse, cross_blocks, panel_weight)

    return jax.shard_map(
        step,
        mesh=mesh,
        in_specs=(
            P(("farm", "body"), None, None, None),
            P(("farm", "body"), None, None, None),
            P(("farm", "body"), None, None, None, None),
            P(("farm", "body"), None),
            P(("farm", "body"), None),
        ),
        out_specs=(P(("farm", "body"), None, None, None), P("farm", None, None)),
        check_vma=False,
    )
```

```python
import functools

import jax
import jax.numpy as jnp
from jax import lax
from jax.experimental import pallas as pl
from jax.experimental.pallas import tpu as pltpu
from jax.sharding import PartitionSpec as P

ITERS = 6
PIECES = 2
DIRECT = 2
F32 = jnp.float32
BF16 = jnp.bfloat16


def flip(index, bits):
    bit = 1
    while bit <= bits:
        if bits & bit:
            index = index + bit - 2 * bit * ((index // bit) % 2)
        bit *= 2
    return index


def halves(value):
    high = value.astype(BF16)
    return high, (value - high.astype(F32)).astype(BF16)


def put_field(lhs, column, value, heads):
    rows, panels = value.shape
    high, low = halves(value)
    high_t = jnp.concatenate([-high[heads:], high[:heads]], axis=0)
    low_t = jnp.concatenate([-low[heads:], low[:heads]], axis=0)
    lhs[0:rows, column : column + panels] = high
    lhs[rows : 2 * rows, column : column + panels] = low
    lhs[0:rows, column + panels : column + 2 * panels] = high_t
    lhs[rows : 2 * rows, column + panels : column + 2 * panels] = low_t


def multiply(lhs, depth, high, low, out, rows):
    panels = out.shape[1]
    tile = 256
    for start in range(0, panels, tile):
        at = slice(start, start + tile)
        both = jnp.dot(lhs[:, 0:depth], high[:, at], preferred_element_type=F32)
        small = jnp.dot(lhs[0:rows, 0:depth], low[:, at], preferred_element_type=F32)
        out[:, start : start + tile] = both[:rows] + both[rows:] + small


def kernel(
    bodies, slots, heads, panels,
    neighbours, incident, inverse, blocks, weight,
    out, force,
    stage, inv_high, inv_low, cross_high, cross_low, even, odd, lhs, product, shares,
    load_sem, send_sem, recv_sem, share_send, share_recv,
):
    rows = 2 * heads
    me = lax.axis_index("body")
    depth_z = bodies // 4
    gathered = (even, odd)

    def load(index):
        source = inverse.at[0, index] if index < 2 else blocks.at[0, (index - 2) // 2, (index - 2) % 2]
        return pltpu.make_async_copy(source, stage.at[index], load_sem.at[index])

    for index in range(2 + 2 * slots):
        load(index).start()

    barrier = pltpu.get_barrier_semaphore()
    for bits in range(1, bodies):
        pl.semaphore_signal(barrier, inc=1, device_id={"body": flip(me, bits)})

    def split(index, high, low, base):
        load(index).wait()

        @pl.loop(0, panels // 128)
        def _(step):
            at = pl.ds(pl.multiple_of(step * 128, 128), 128)
            upper, lower = halves(stage[index, at, :].T)
            high[base : base + panels, at] = upper
            low[base : base + panels, at] = lower

    z = me // 4

    def at_z(steps, act):
        if steps > 0:
            pl.when(z + steps < depth_z)(act)
        else:
            pl.when(z + steps >= 0)(act)

    def send(parity, slot, target, kind, mark, piece):
        part = pl.ds(piece * (rows // PIECES), rows // PIECES)
        return pltpu.make_async_remote_copy(
            src_ref=gathered[parity].at[slot, part],
            dst_ref=gathered[parity].at[slot, part],
            send_sem=send_sem.at[kind, mark, piece],
            recv_sem=recv_sem.at[parity, slot, piece],
            device_id={"body": target},
        )

    def wait_in(parity, slot, piece):
        send(parity, slot, flip(me, 1), 0, slot, piece).wait_recv()

    def to_core(parity, slot, piece):
        return send(parity, slot, flip(me, 1), 0, slot, piece)

    def to_row(parity, slot, piece):
        return send(parity, slot, flip(me, 2), 1, slot, piece)

    def own_sends(parity, act):
        for steps in range(1, DIRECT + 1):
            for piece in range(PIECES):
                for way in (steps, -steps):
                    target = me + 4 * way
                    at_z(way, lambda target=target, piece=piece: act(send(parity, me, target, 3, target, piece)))
                if steps == 1:
                    act(to_row(parity, me, piece))
        for piece in range(PIECES):
            act(to_core(parity, me, piece))

    def column(parity, steps, arrive, act):
        for piece in range(PIECES):
            for way in (steps, -steps):
                def one(way=way, piece=piece):
                    slot = me + 4 * way
                    if arrive:
                        wait_in(parity, slot, piece)
                    if steps >= DIRECT:
                        on = -1 if way > 0 else 1
                        at_z(on, lambda: act(send(parity, slot, me + 4 * on, 2, slot, piece)))
                    act(to_row(parity, slot, piece))
                    act(to_core(parity, slot, piece))
                at_z(way, one)

    def other(parity, steps, arrive, act):
        for piece in range(PIECES):
            for way in {steps: None, -steps: None}:
                def one(way=way, piece=piece):
                    slot = flip(me, 2) + 4 * way
                    if arrive:
                        wait_in(parity, slot, piece)
                    act(to_core(parity, slot, piece))
                if way:
                    at_z(way, one)
                else:
                    one()

    def start(copy):
        copy.start()

    def wait_send(copy):
        copy.wait_send()

    def start_own(parity):
        own_sends(parity, start)

    def relays(parity, arrive, act):
        for steps in range(depth_z):
            if steps:
                column(parity, steps, arrive, act)
            if steps > 1:
                other(parity, steps - 2, arrive, act)
        for steps in range(max(depth_z - 2, 0), depth_z):
            other(parity, steps, arrive, act)

    def finish_gather(parity):
        relays(parity, True, start)
        for plane in range(depth_z):
            for row in range(2):
                for piece in range(PIECES):
                    wait_in(parity, 4 * plane + 2 * row + 1 - me % 2, piece)

    def wait_sends(parity):
        own_sends(parity, wait_send)
        relays(parity, False, wait_send)

    field = incident[0].reshape(rows, panels)
    for part in range(2):
        split(part, inv_high, inv_low, part * panels)
    put_field(lhs, 0, field, heads)
    multiply(lhs, 2 * panels, inv_high, inv_low, product, rows)
    even[me] = product[...]
    pl.semaphore_wait(barrier, bodies - 1)
    start_own(0)
    for part in range(2 * slots):
        split(2 + part, cross_high, cross_low, part * panels)

    def sweep(parity):
        finish_gather(parity)
        for slot in range(slots):
            name = neighbours[0, slot]
            value = gathered[parity][jnp.maximum(name, 0)]
            put_field(lhs, 2 * slot * panels, jnp.where(name >= 0, value, 0.0), heads)
        multiply(lhs, 2 * slots * panels, cross_high, cross_low, product, rows)
        put_field(lhs, 0, incident[0].reshape(rows, panels) - product[...], heads)
        multiply(lhs, 2 * panels, inv_high, inv_low, product, rows)
        wait_sends(parity)

    @pl.loop(0, ITERS // 2)
    def _(pair):
        sweep(0)
        odd[me] = product[...]
        start_own(1)
        sweep(1)

        @pl.when(pair < ITERS // 2 - 1)
        def _():
            even[me] = product[...]
            start_own(0)

    final = product[...]
    out[0] = final.reshape(2, heads, panels)
    scale = jnp.broadcast_to(weight[...], (8, panels))
    sums = [
        lax.dot_general(
            scale, final[c * heads : (c + 1) * heads], (((1,), (1,)), ((), ())),
            precision=lax.Precision.HIGHEST, preferred_element_type=F32,
        )
        for c in range(2)
    ]
    row = lax.broadcasted_iota(jnp.int32, (8, heads), 0)
    shares[me] = jnp.zeros((8, 128), F32)
    shares[me, :, 0:heads] = jnp.where(row == 0, sums[0], sums[1])

    def share(bits):
        return pltpu.make_async_remote_copy(
            src_ref=shares.at[me],
            dst_ref=shares.at[me],
            send_sem=share_send.at[bits],
            recv_sem=share_recv.at[bits],
            device_id={"body": flip(me, bits)},
        )

    def share_in(bits):
        slot = flip(me, bits)
        return pltpu.make_async_remote_copy(
            src_ref=shares.at[slot],
            dst_ref=shares.at[slot],
            send_sem=share_send.at[bits],
            recv_sem=share_recv.at[bits],
            device_id={"body": slot},
        )

    for bits in range(1, bodies):
        share(bits).start()
    for bits in range(1, bodies):
        share_in(bits).wait_recv()
    total = shares[0]
    for other in range(1, bodies):
        total = total + shares[other]
    force[0] = total[0:2, 0:heads]
    for bits in range(1, bodies):
        share(bits).wait_send()


def solution(mesh):
    bodies = mesh.shape["body"]

    def step(incident, self_inverse, cross_blocks, neighbours, panel_weight):
        heads, panels = incident.shape[2:]
        slots = neighbours.shape[1]
        rows = 2 * heads
        vmem = pl.BlockSpec(memory_space=pltpu.VMEM)
        anywhere = pl.BlockSpec(memory_space=pl.ANY)
        return pl.pallas_call(
            functools.partial(kernel, bodies, slots, heads, panels),
            out_shape=(
                jax.ShapeDtypeStruct(incident.shape, F32),
                jax.ShapeDtypeStruct((1, 2, heads), F32),
            ),
            in_specs=[pl.BlockSpec(memory_space=pltpu.SMEM), vmem, anywhere, anywhere, vmem],
            out_specs=(vmem, vmem),
            scratch_shapes=[
                pltpu.VMEM((2 + 2 * slots, panels, panels), F32),
                pltpu.VMEM((2 * panels, panels), BF16),
                pltpu.VMEM((2 * panels, panels), BF16),
                pltpu.VMEM((2 * slots * panels, panels), BF16),
                pltpu.VMEM((2 * slots * panels, panels), BF16),
                pltpu.VMEM((bodies, rows, panels), F32),
                pltpu.VMEM((bodies, rows, panels), F32),
                pltpu.VMEM((2 * rows, 2 * slots * panels), BF16),
                pltpu.VMEM((rows, panels), F32),
                pltpu.VMEM((bodies, 8, 128), F32),
                pltpu.SemaphoreType.DMA((2 + 2 * slots,)),
                pltpu.SemaphoreType.DMA((4, bodies, PIECES)),
                pltpu.SemaphoreType.DMA((2, bodies, PIECES)),
                pltpu.SemaphoreType.DMA((bodies,)),
                pltpu.SemaphoreType.DMA((bodies,)),
            ],
            compiler_params=pltpu.CompilerParams(
                collective_id=0, has_side_effects=True, vmem_limit_bytes=60 * 1024 * 1024
            ),
        )(neighbours, incident, self_inverse, cross_blocks, panel_weight)

    return jax.shard_map(
        step,
        mesh=mesh,
        in_specs=(
            P(("farm", "body"), None, None, None),
            P(("farm", "body"), None, None, None),
            P(("farm", "body"), None, None, None, None),
            P(("farm", "body"), None),
            P(("farm", "body"), None),
        ),
        out_specs=(P(("farm", "body"), None, None, None), P("farm", None, None)),
        check_vma=False,
    )
```

```python
import functools

import jax
import jax.numpy as jnp
from jax import lax
from jax.experimental import pallas as pl
from jax.experimental.pallas import tpu as pltpu
from jax.sharding import PartitionSpec as P

ITERS = 6
PIECES = 2
FIRST = 1
DIRECT = 2
F32 = jnp.float32
BF16 = jnp.bfloat16


def flip(index, bits):
    bit = 1
    while bit <= bits:
        if bits & bit:
            index = index + bit - 2 * bit * ((index // bit) % 2)
        bit *= 2
    return index


def pieces(panels):
    first = FIRST * panels // 3
    return [(0, first), (first, panels - first)]


def halves(value):
    high = value.astype(BF16)
    return high, (value - high.astype(F32)).astype(BF16)


def put_field(lhs, column, value, heads):
    rows, width = value.shape
    high, low = halves(value)
    high_t = jnp.concatenate([-high[heads:], high[:heads]], axis=0)
    low_t = jnp.concatenate([-low[heads:], low[:heads]], axis=0)
    lhs[0:rows, column : column + width] = high
    lhs[rows : 2 * rows, column : column + width] = low
    lhs[0:rows, column + width : column + 2 * width] = high_t
    lhs[rows : 2 * rows, column + width : column + 2 * width] = low_t


def multiply(lhs, base, depth, high, low, at, rows):
    deep = slice(base, base + depth)
    both = jnp.dot(lhs[:, 0:depth], high[deep, at], preferred_element_type=F32)
    small = jnp.dot(lhs[0:rows, 0:depth], low[deep, at], preferred_element_type=F32)
    return both[:rows] + both[rows:] + small


def kernel(
    bodies, slots, heads, panels,
    neighbours, incident, inverse, blocks, weight,
    out, force,
    stage, inv_high, inv_low, cross_high, cross_low, lhs, product, shares,
    load_sem, send_sem, recv_sem, share_send, share_recv, *buffers,
):
    rows = 2 * heads
    me = lax.axis_index("body")
    depth_z = bodies // 4
    gathered = (buffers[:PIECES], buffers[PIECES:])
    cuts = [slice(start, start + width) for start, width in pieces(panels)]
    widths = [width for _, width in pieces(panels)]
    tiles = [slice(start, start + 256) for start in range(0, panels, 256)]

    def load(index):
        source = inverse.at[0, index] if index < 2 else blocks.at[0, (index - 2) // 2, (index - 2) % 2]
        return pltpu.make_async_copy(source, stage.at[index], load_sem.at[index])

    for index in range(2 + 2 * slots):
        load(index).start()

    barrier = pltpu.get_barrier_semaphore()
    for bits in range(1, bodies):
        pl.semaphore_signal(barrier, inc=1, device_id={"body": flip(me, bits)})

    def split(index, high, low, part, parts):
        load(index).wait()

        @pl.loop(0, panels // 128)
        def _(step):
            at = pl.ds(pl.multiple_of(step * 128, 128), 128)
            upper, lower = halves(stage[index, at, :].T)
            for piece, cut in enumerate(cuts):
                to = parts * cut.start + part * widths[piece]
                high[to : to + widths[piece], at] = upper[cut]
                low[to : to + widths[piece], at] = lower[cut]

    z = me // 4

    def at_z(steps, act):
        if steps > 0:
            pl.when(z + steps < depth_z)(act)
        else:
            pl.when(z + steps >= 0)(act)

    def send(parity, slot, target, kind, mark, piece):
        return pltpu.make_async_remote_copy(
            src_ref=gathered[parity][piece].at[slot],
            dst_ref=gathered[parity][piece].at[slot],
            send_sem=send_sem.at[kind, mark, piece],
            recv_sem=recv_sem.at[parity, slot, piece],
            device_id={"body": target},
        )

    def wait_in(parity, slot, piece):
        send(parity, slot, flip(me, 1), 0, slot, piece).wait_recv()

    def to_core(parity, slot, piece):
        return send(parity, slot, flip(me, 1), 0, slot, piece)

    def to_row(parity, slot, piece):
        return send(parity, slot, flip(me, 2), 1, slot, piece)

    def own_sends(parity, piece, act):
        for steps in range(1, DIRECT + 1):
            for way in (steps, -steps):
                target = me + 4 * way
                at_z(way, lambda target=target: act(send(parity, me, target, 3, target, piece)))
            if steps == 1:
                act(to_row(parity, me, piece))
        act(to_core(parity, me, piece))

    def column(parity, steps, piece, arrive, act):
        for way in (steps, -steps):
            def one(way=way):
                slot = me + 4 * way
                if arrive:
                    wait_in(parity, slot, piece)
                if steps >= DIRECT:
                    on = -1 if way > 0 else 1
                    at_z(on, lambda: act(send(parity, slot, me + 4 * on, 2, slot, piece)))
                act(to_row(parity, slot, piece))
                act(to_core(parity, slot, piece))
            at_z(way, one)

    def other(parity, steps, piece, arrive, act):
        for way in {steps: None, -steps: None}:
            def one(way=way):
                slot = flip(me, 2) + 4 * way
                if arrive:
                    wait_in(parity, slot, piece)
                act(to_core(parity, slot, piece))
            if way:
                at_z(way, one)
            else:
                one()

    def start(copy):
        copy.start()

    def wait_send(copy):
        copy.wait_send()

    def relay_column(parity, piece):
        for steps in range(1, depth_z):
            column(parity, steps, piece, True, start)
            if steps > 1:
                other(parity, steps - 2, piece, True, start)

    def relay_other(parity, piece):
        for steps in range(max(depth_z - 2, 0), depth_z):
            other(parity, steps, piece, True, start)
        for plane in range(depth_z):
            for row in range(2):
                wait_in(parity, 4 * plane + 2 * row + 1 - me % 2, piece)

    def wait_sends(parity):
        for piece in range(PIECES):
            own_sends(parity, piece, wait_send)
            for steps in range(depth_z):
                if steps:
                    column(parity, steps, piece, False, wait_send)
                other(parity, steps, piece, False, wait_send)

    def solve(parity, value):
        for piece, cut in enumerate(cuts):
            put_field(lhs, 2 * cut.start, value[:, cut], heads)
        for piece, cut in enumerate(cuts):
            part = multiply(lhs, 0, 2 * panels, inv_high, inv_low, cut, rows)
            if parity is None:
                product[:, cut] = part
            else:
                gathered[parity][piece][me] = part
                own_sends(parity, piece, start)

    for part in range(2):
        split(part, inv_high, inv_low, part, 2)
    pl.semaphore_wait(barrier, bodies - 1)
    solve(0, incident[0].reshape(rows, panels))
    for part in range(2 * slots):
        split(2 + part, cross_high, cross_low, part, 2 * slots)

    def sweep(parity):
        for piece in range(PIECES):
            relay_column(parity, piece)
            if piece > 0:
                consume(parity, piece - 1)
        consume(parity, PIECES - 1)
        wait_sends(parity)

    def consume(parity, piece):
        relay_other(parity, piece)
        for slot in range(slots):
            name = neighbours[0, slot]
            value = gathered[parity][piece][jnp.maximum(name, 0)]
            put_field(lhs, 2 * slot * widths[piece], jnp.where(name >= 0, value, 0.0), heads)
        depth = 2 * slots * widths[piece]
        for cut in tiles:
            part = multiply(lhs, 2 * slots * cuts[piece].start, depth, cross_high, cross_low, cut, rows)
            before = incident[0, :, :, cut].reshape(rows, 256) if piece == 0 else product[:, cut]
            product[:, cut] = before - part

    @pl.loop(0, ITERS // 2)
    def _(pair):
        sweep(0)
        solve(1, product[...])
        sweep(1)

        @pl.when(pair < ITERS // 2 - 1)
        def _():
            solve(0, product[...])

    solve(None, product[...])
    final = product[...]
    out[0] = final.reshape(2, heads, panels)
    scale = jnp.broadcast_to(weight[...], (8, panels))
    sums = [
        lax.dot_general(
            scale, final[c * heads : (c + 1) * heads], (((1,), (1,)), ((), ())),
            precision=lax.Precision.HIGHEST, preferred_element_type=F32,
        )
        for c in range(2)
    ]
    row = lax.broadcasted_iota(jnp.int32, (8, heads), 0)
    shares[me] = jnp.zeros((8, 128), F32)
    shares[me, :, 0:heads] = jnp.where(row == 0, sums[0], sums[1])

    def share(bits):
        return pltpu.make_async_remote_copy(
            src_ref=shares.at[me],
            dst_ref=shares.at[me],
            send_sem=share_send.at[bits],
            recv_sem=share_recv.at[bits],
            device_id={"body": flip(me, bits)},
        )

    def share_in(bits):
        slot = flip(me, bits)
        return pltpu.make_async_remote_copy(
            src_ref=shares.at[slot],
            dst_ref=shares.at[slot],
            send_sem=share_send.at[bits],
            recv_sem=share_recv.at[bits],
            device_id={"body": slot},
        )

    for bits in range(1, bodies):
        share(bits).start()
    for bits in range(1, bodies):
        share_in(bits).wait_recv()
    total = shares[0]
    for other in range(1, bodies):
        total = total + shares[other]
    force[0] = total[0:2, 0:heads]
    for bits in range(1, bodies):
        share(bits).wait_send()


def solution(mesh):
    bodies = mesh.shape["body"]

    def step(incident, self_inverse, cross_blocks, neighbours, panel_weight):
        heads, panels = incident.shape[2:]
        slots = neighbours.shape[1]
        rows = 2 * heads
        vmem = pl.BlockSpec(memory_space=pltpu.VMEM)
        anywhere = pl.BlockSpec(memory_space=pl.ANY)
        return pl.pallas_call(
            functools.partial(kernel, bodies, slots, heads, panels),
            out_shape=(
                jax.ShapeDtypeStruct(incident.shape, F32),
                jax.ShapeDtypeStruct((1, 2, heads), F32),
            ),
            in_specs=[pl.BlockSpec(memory_space=pltpu.SMEM), vmem, anywhere, anywhere, vmem],
            out_specs=(vmem, vmem),
            scratch_shapes=[
                pltpu.VMEM((2 + 2 * slots, panels, panels), F32),
                pltpu.VMEM((2 * panels, panels), BF16),
                pltpu.VMEM((2 * panels, panels), BF16),
                pltpu.VMEM((2 * slots * panels, panels), BF16),
                pltpu.VMEM((2 * slots * panels, panels), BF16),
                pltpu.VMEM((2 * rows, 2 * slots * panels), BF16),
                pltpu.VMEM((rows, panels), F32),
                pltpu.VMEM((bodies, 8, 128), F32),
                pltpu.SemaphoreType.DMA((2 + 2 * slots,)),
                pltpu.SemaphoreType.DMA((4, bodies, PIECES)),
                pltpu.SemaphoreType.DMA((2, bodies, PIECES)),
                pltpu.SemaphoreType.DMA((bodies,)),
                pltpu.SemaphoreType.DMA((bodies,)),
                *[pltpu.VMEM((bodies, rows, width), F32) for _, width in pieces(panels)] * 2,
            ],
            compiler_params=pltpu.CompilerParams(
                collective_id=0, has_side_effects=True, vmem_limit_bytes=60 * 1024 * 1024
            ),
        )(neighbours, incident, self_inverse, cross_blocks, panel_weight)

    return jax.shard_map(
        step,
        mesh=mesh,
        in_specs=(
            P(("farm", "body"), None, None, None),
            P(("farm", "body"), None, None, None),
            P(("farm", "body"), None, None, None, None),
            P(("farm", "body"), None),
            P(("farm", "body"), None),
        ),
        out_specs=(P(("farm", "body"), None, None, None), P("farm", None, None)),
        check_vma=False,
    )
```
